32 devices in a mesh: groups: 2 (over y), seq: 8 (over z, x), head: 2 (over core).
Axes of the slice: x: 2, y: 2, z: 4, core: 2. Of those that a mesh axis runs over, the one named last changes fastest.
Arguments:
- queries: bfloat16 [4096, 2048], P(('groups', 'seq'), 'head'), parts along dimension 0, may hold values from -24 to 24
- keys: bfloat16 [4096, 2048], P(('groups', 'seq'), 'head'), parts along dimension 0, may hold values from -24 to 24
- values: bfloat16 [4096, 2048], P(('groups', 'seq'), 'head'), parts along dimension 0, may hold values from -6 to 6
Outputs:
- attended: bfloat16 [4096, 2048], P(('groups', 'seq'), 'head'), parts along dimension 0
The draws below stay inside these ranges and needn't reach their ends.
There are 2 independent parts, one for each index of `groups`. The reference program is written for one: setup_inputs(seed, part) draws one part's arguments, and reference() takes and returns one part's arrays. A program takes and returns all parts, laid end to end along the dimension named above; each array names one. Nothing has to cross between parts.
All inputs are finite; a program needn't handle non-finite values.
Results may differ from the reference program's by a relative error of at most 0.0057.
Values may be sent and summed in bfloat16 or wider, within the bound.
A program may use at most 64 MiB of HBM per device.

```python
import jax
import jax.numpy as jnp
from jax import lax

HEADS = 16
HEAD_DIM = 128
D = 2048
BLOCK = 128
TOKENS = 2048
LEVELS = 3


def draw_queries(key, part):
    key = jax.random.fold_in(key, 11)
    first = jax.random.fold_in(key, 0)
    fresh = jax.random.normal(first, (TOKENS, D), jnp.float32)
    return jnp.clip(fresh, -6.0, 6.0).astype(jnp.bfloat16)


def draw_keys(key, part):
    key = jax.random.fold_in(key, 23)
    first = jax.random.fold_in(key, 0)
    fresh = jax.random.normal(first, (TOKENS, D), jnp.float32)
    return jnp.clip(fresh, -6.0, 6.0).astype(jnp.bfloat16)


def level_of(stream_key, dims, cuts, least, high):
    def one(axis_at, parts):
        draws = jax.random.uniform(jax.random.fold_in(jax.random.fold_in(stream_key, 6), axis_at), (parts,), jnp.float32, least / len(cuts), high / len(cuts))
        return jnp.repeat(jnp.exp(draws), dims[axis_at] // parts).reshape((-1,) + (1,) * (len(dims) - axis_at - 1))

    level = one(*cuts[0])
    for cut in cuts[1:]:
        level = level * one(*cut)
    return level


def gaussian(own_key, extent, width, limit, cuts=(), kind=jnp.bfloat16):
    values = width * jax.random.normal(own_key, extent, jnp.float32)
    if cuts:
        values = values * level_of(own_key, extent, cuts, -0.22, 0.18)
    return jnp.clip(values, -limit, limit).astype(kind)


def setup_inputs(seed: int = 0, part: int = 0) -> dict:
    arg_keys = jax.random.split(jax.random.key(seed), 4)
    part_keys = jax.random.split(jax.random.fold_in(arg_keys[3], part), 4)
    return {
        "queries": draw_queries(jax.random.fold_in(jax.random.fold_in(arg_keys[3], part), 71), part),
        "keys": draw_keys(jax.random.fold_in(jax.random.fold_in(arg_keys[3], part), 71), part),
        "values": gaussian(part_keys[2], (TOKENS, D), 1.0, 6.0, ((0, 8), (1, 2))),
    }


def pair_mean(x):
    shape = x.shape
    y = x.reshape(shape[:-3] + (shape[-3] // 2, 2) + shape[-2:]).astype(jnp.float32)
    return ((y[..., 0, :, :] + y[..., 1, :, :]) * 0.5).astype(jnp.bfloat16)


def attend(query_blk, key_blk, value_blk, keep):
    scale = 1.0 / (HEAD_DIM ** 0.5)
    scores = jnp.einsum("nqhe,nkhe->nqhk", query_blk.astype(jnp.float32), key_blk.astype(jnp.float32), precision=lax.Precision.HIGHEST) * scale
    if keep is not None:
        scores = jnp.where(keep[:, None, None, :], scores, -1e30)
    top = jnp.max(scores, axis=-1)
    probs = jnp.exp(scores - top[..., None])
    denom = jnp.sum(probs, axis=-1)
    numer = jnp.einsum("nqhk,nkhe->nqhe", probs.astype(jnp.bfloat16).astype(jnp.float32), value_blk.astype(jnp.float32), precision=lax.Precision.HIGHEST)
    heads = query_blk.shape[2]
    return top.reshape(-1, heads), denom.reshape(-1, heads), numer.reshape(-1, heads, HEAD_DIM)


def one_head(query_h, key_h, value_h):
    total = query_h.shape[0]
    count = total // BLOCK
    qh = query_h.reshape(total, 1, HEAD_DIM)
    kv = jnp.stack([key_h, value_h]).reshape(2, total, 1, HEAD_DIM)
    zero_blk = jnp.zeros((2, BLOCK, 1, HEAD_DIM), jnp.bfloat16)
    padded = jnp.concatenate([zero_blk, kv, zero_blk], axis=1).reshape(2, count + 2, BLOCK, 1, HEAD_DIM)
    window = jnp.concatenate([padded[:, :-2], padded[:, 1:-1], padded[:, 2:]], axis=2)
    blockid = jnp.arange(count)[:, None]
    column = jnp.arange(3 * BLOCK)[None, :]
    keep = jnp.logical_not(((blockid == 0) & (column < BLOCK)) | ((blockid == count - 1) & (column >= 2 * BLOCK)))
    results = [attend(qh.reshape(count, BLOCK, 1, HEAD_DIM), window[0], window[1], keep)]
    level_q = qh
    level_kv = kv
    for level in range(1, LEVELS + 1):
        level_q = pair_mean(level_q)
        level_kv = pair_mean(level_kv)
        nblk = level_q.shape[0] // BLOCK
        qblk = level_q.reshape(nblk, BLOCK, 1, HEAD_DIM)
        sibling = level_kv.reshape(2, nblk // 2, 2, BLOCK, 1, HEAD_DIM)[:, :, ::-1].reshape(2, nblk, BLOCK, 1, HEAD_DIM)
        results.append(attend(qblk, sibling[0], sibling[1], None))
    expanded = []
    for level, (top, denom, numer) in enumerate(results):
        factor = 2 ** level
        expanded.append((jnp.repeat(top, factor, axis=0), jnp.repeat(denom, factor, axis=0), jnp.repeat(numer, factor, axis=0)))
    highest = expanded[0][0]
    for item in expanded[1:]:
        highest = jnp.maximum(highest, item[0])
    numer_all = jnp.zeros((total, 1, HEAD_DIM), jnp.float32)
    denom_all = jnp.zeros((total, 1), jnp.float32)
    for level, (top, denom, numer) in enumerate(expanded):
        weight = (2.0 ** level) * jnp.exp(top - highest)
        numer_all = numer_all + weight[..., None] * numer
        denom_all = denom_all + weight * denom
    return (numer_all / denom_all[..., None]).astype(jnp.bfloat16).reshape(total, HEAD_DIM)


def reference(queries, keys, values):
    def per_head(head_id):
        start = (head_id * HEAD_DIM).astype(jnp.int32)
        return one_head(lax.dynamic_slice_in_dim(queries, start, HEAD_DIM, 1), lax.dynamic_slice_in_dim(keys, start, HEAD_DIM, 1), lax.dynamic_slice_in_dim(values, start, HEAD_DIM, 1))

    outputs = lax.map(per_head, jnp.arange(HEADS, dtype=jnp.int32))
    return jnp.transpose(outputs, (1, 0, 2)).reshape(queries.shape[0], HEADS * HEAD_DIM)
```

```python
import functools
import math

import jax
import jax.numpy as jnp
from jax import lax
from jax.experimental import pallas as pl
from jax.experimental.pallas import tpu as pltpu
from jax.sharding import PartitionSpec as P

HEAD_DIM = 128
BLOCK = 128
MAX_LEVELS = 7
MESH = pl.DeviceIdType.MESH
RATE = math.log2(math.e) / math.sqrt(HEAD_DIM)


def softmax_part(scores, value):
    top = jnp.max(scores, axis=1, keepdims=True)
    probs = jnp.exp2((scores - top) * RATE).astype(jnp.bfloat16)
    wide = jnp.concatenate([value, jnp.ones_like(value)], axis=1)
    both = jnp.dot(probs, wide, preferred_element_type=jnp.float32)
    return top, both


def score(query, key):
    return lax.dot_general(
        query, key, (((1,), (1,)), ((), ())), preferred_element_type=jnp.float32
    )


def kernel(
    pairs, levels, local, q_in, k_in, v_in, out, kv, qbuf, obuf, kv1, own, sib,
    state, load_sem, kv_send, kv_recv, q_send, q_recv, halo_send, halo_recv,
    lev_send, lev_recv, out_local, out_send, out_recv,
):
    rows, width = q_in.shape
    half = width // 2
    heads = half // HEAD_DIM
    total = 2 * rows
    blocks = total // BLOCK
    place = lax.axis_index("seq")
    side = lax.rem(place, 2)
    other = 1 - side
    pair = place // 2
    partner = {"seq": pair * 2 + other}
    below = {"seq": lax.rem(pair + pairs - 1, pairs) * 2 + side}
    above = {"seq": lax.rem(pair + 1, pairs) * 2 + side}

    def mirror(level):
        apart = 1 << (level - local)
        bit = lax.rem(pair // apart, 2)
        return {"seq": (pair + apart - 2 * apart * bit) * 2 + side}

    barrier = pltpu.get_barrier_semaphore()
    peers = [partner, below, above] + [mirror(l) for l in range(local, levels + 1)]
    for peer in peers:
        pl.semaphore_signal(barrier, inc=1, device_id=peer, device_id_type=MESH)

    mine = pl.ds(pl.multiple_of(side * half, half), half)
    own_rows = pl.ds(pl.multiple_of(BLOCK + side * rows, BLOCK), rows)
    q_rows = pl.ds(pl.multiple_of(side * rows, BLOCK), rows)
    loads = [
        pltpu.make_async_copy(k_in.at[:, mine], kv.at[0, own_rows], load_sem.at[0]),
        pltpu.make_async_copy(v_in.at[:, mine], kv.at[1, own_rows], load_sem.at[1]),
        pltpu.make_async_copy(q_in.at[:, mine], qbuf.at[q_rows], load_sem.at[2]),
    ]
    for load in loads:
        load.start()
    pl.semaphore_wait(barrier, len(peers))

    def lanes(h):
        return pl.ds(pl.multiple_of(h * HEAD_DIM, HEAD_DIM), HEAD_DIM)

    def remote(src, dst, send, recv, device):
        return pltpu.make_async_remote_copy(
            src_ref=src, dst_ref=dst, send_sem=send, recv_sem=recv,
            device_id=device, device_id_type=MESH,
        )

    def theirs(h):
        return pl.ds(pl.multiple_of(other * half + h * HEAD_DIM, HEAD_DIM), HEAD_DIM)

    def send_k(h):
        return remote(k_in.at[:, theirs(h)], kv.at[0, own_rows, lanes(h)],
                      kv_send.at[0, h], kv_recv.at[0, h], partner)

    def send_v(h):
        return remote(v_in.at[:, theirs(h)], kv.at[1, own_rows, lanes(h)],
                      kv_send.at[1, h], kv_recv.at[1, h], partner)

    def send_q(h):
        return remote(q_in.at[:, theirs(h)], qbuf.at[q_rows, lanes(h)],
                      q_send.at[h], q_recv.at[h], partner)

    def send_down(h):
        return remote(kv.at[:, pl.ds(BLOCK, BLOCK), lanes(h)],
                      kv.at[:, pl.ds(BLOCK + total, BLOCK), lanes(h)],
                      halo_send.at[0, h], halo_recv.at[0, h], below)

    def send_up(h):
        return remote(kv.at[:, pl.ds(total, BLOCK), lanes(h)],
                      kv.at[:, pl.ds(0, BLOCK), lanes(h)],
                      halo_send.at[1, h], halo_recv.at[1, h], above)

    def send_level(level, h):
        at = level - local
        return remote(own.at[at, :, :, lanes(h)], sib.at[at, :, :, lanes(h)],
                      lev_send.at[at, h], lev_recv.at[at, h], mirror(level))

    def keep_out(h):
        cols = pl.ds(pl.multiple_of(side * half + h * HEAD_DIM, HEAD_DIM), HEAD_DIM)
        return pltpu.make_async_copy(
            obuf.at[q_rows, lanes(h)], out.at[:, cols], out_local.at[h])

    def send_out(h):
        cols = pl.ds(pl.multiple_of(side * half + h * HEAD_DIM, HEAD_DIM), HEAD_DIM)
        far = pl.ds(pl.multiple_of(other * rows, BLOCK), rows)
        return remote(obuf.at[far, lanes(h)], out.at[:, cols],
                      out_send.at[h], out_recv.at[h], partner)

    def each(body):
        @pl.loop(0, heads)
        def _(h):
            body(h)

    def start_kv(h):
        send_k(h).start()
        send_v(h).start()

    each(start_kv)
    each(lambda h: send_q(h).start())

    first, last = pair == 0, pair == pairs - 1

    @pl.when(first)
    def _():
        kv[:, pl.ds(0, BLOCK), :] = jnp.zeros((2, BLOCK, half), kv.dtype)

    @pl.when(last)
    def _():
        kv[:, pl.ds(BLOCK + total, BLOCK), :] = jnp.zeros((2, BLOCK, half), kv.dtype)

    loads[0].wait()
    loads[1].wait()

    def halo(h, here):
        @pl.when((side == here) & jnp.logical_not(first))
        def _():
            send_down(h).start()

        @pl.when((side == 1 - here) & jnp.logical_not(last))
        def _():
            send_up(h).start()

    each(lambda h: halo(h, 0))

    rowid = lax.broadcasted_iota(jnp.int32, (BLOCK, 2 * BLOCK), 0)
    colid = lax.broadcasted_iota(jnp.int32, (BLOCK, 2 * BLOCK), 1)
    averaging = jnp.where((colid >> 1) == rowid, 0.5, 0.0).astype(jnp.bfloat16)

    def mean(x):
        count = x.shape[0]
        parts = []
        for at in range(0, count, 2 * BLOCK):
            size = min(2 * BLOCK, count - at)
            parts.append(
                jnp.dot(averaging[: size // 2, :size], x[at : at + size],
                        preferred_element_type=jnp.float32).astype(jnp.bfloat16)
            )
        return parts[0] if len(parts) == 1 else jnp.concatenate(parts, axis=0)

    def coarsen(h):
        send_k(h).wait_recv()
        send_v(h).wait_recv()
        halo(h, 1)
        both = jnp.concatenate(
            [kv[0, pl.ds(BLOCK, total), lanes(h)], kv[1, pl.ds(BLOCK, total), lanes(h)]],
            axis=1)
        offset = 0
        for level in range(1, local):
            both = mean(both)
            count = total >> level
            for t in range(2):
                kv1[t, pl.ds(offset, count), lanes(h)] = both[:, t * HEAD_DIM : (t + 1) * HEAD_DIM]
            offset += count
        both = mean(both)
        for t in range(2):
            own[0, t, :, lanes(h)] = both[:, t * HEAD_DIM : (t + 1) * HEAD_DIM]
        send_level(local, h).start()

    each(coarsen)

    for level in range(local, levels):
        at = level - local

        def climb(h, level=level, at=at):
            send_level(level, h).wait_recv()
            for t in range(2):
                joined = jnp.concatenate([own[at, t, :, lanes(h)], sib[at, t, :, lanes(h)]], axis=0)
                own[at + 1, t, :, lanes(h)] = mean(joined)
            send_level(level + 1, h).start()

        each(climb)

    loads[2].wait()

    def attend(h):
        send_q(h).wait_recv()
        send_level(levels, h).wait_recv()

        @pl.when(jnp.logical_not(last))
        def _():
            send_down(h).wait_recv()

        @pl.when(jnp.logical_not(first))
        def _():
            send_up(h).wait_recv()

        queries = [qbuf[:, lanes(h)]]
        for level in range(1, levels + 1):
            queries.append(mean(queries[-1]))

        found = None
        for level in range(levels, -1, -1):
            count = total >> level
            if level >= local:
                at = level - local
                tops, both = softmax_part(
                    score(queries[level], sib[at, 0, :, lanes(h)]), sib[at, 1, :, lanes(h)])
                pieces = [(0, count, tops, both)]
            elif level >= 1:
                offset = sum(total >> l for l in range(1, level))
                pieces = []
                for b in range(count // BLOCK):
                    near = pl.ds(offset + (b ^ 1) * BLOCK, BLOCK)
                    tops, both = softmax_part(
                        score(queries[level][b * BLOCK : (b + 1) * BLOCK], kv1[0, near, lanes(h)]),
                        kv1[1, near, lanes(h)])
                    pieces.append((b * BLOCK, BLOCK, tops, both))
            else:
                pieces = []
                for b in range(blocks):
                    window = pl.ds(b * BLOCK, 3 * BLOCK)
                    s = score(queries[0][b * BLOCK : (b + 1) * BLOCK], kv[0, window, lanes(h)])
                    if b == 0:
                        s = jnp.concatenate(
                            [jnp.where(first, -1e30, s[:, :BLOCK]), s[:, BLOCK:]], axis=1)
                    if b == blocks - 1:
                        s = jnp.concatenate(
                            [s[:, : 2 * BLOCK], jnp.where(last, -1e30, s[:, 2 * BLOCK :])], axis=1)
                    tops, both = softmax_part(s, kv[1, window, lanes(h)])
                    pieces.append((b * BLOCK, BLOCK, tops, both))
            for start, size, tops, both in pieces:
                num, den = both[:, :HEAD_DIM], both[:, HEAD_DIM:]
                top = jnp.broadcast_to(tops, (size, HEAD_DIM))
                if level < levels:
                    span = pl.ds(start, size)
                    coarse_top = state[level, 0, span, :]
                    highest = jnp.maximum(top, coarse_top)
                    fine_weight = jnp.exp2((top - highest) * RATE)
                    coarse_weight = 2.0 * jnp.exp2((coarse_top - highest) * RATE)
                    top = highest
                    den = fine_weight * den + coarse_weight * state[level, 1, span, :]
                    num = fine_weight * num + coarse_weight * state[level, 2, span, :]
                if level == 0:
                    obuf[pl.ds(start, size), lanes(h)] = (num / den).astype(obuf.dtype)
                else:
                    for at, x in enumerate((top, den, num)):
                        for odd in range(2):
                            state[level - 1, at, pl.ds(2 * start + odd, size, stride=2), :] = x
        keep_out(h).start()
        send_out(h).start()

    each(attend)

    def finish(h):
        send_k(h).wait_send()
        send_v(h).wait_send()
        send_q(h).wait_send()
        for level in range(local, levels + 1):
            send_level(level, h).wait_send()

        @pl.when(jnp.logical_not(first))
        def _():
            send_down(h).wait_send()

        @pl.when(jnp.logical_not(last))
        def _():
            send_up(h).wait_send()

        keep_out(h).wait()
        send_out(h).wait()

    each(finish)


def on_device(queries, keys, values):
    rows, width = queries.shape
    half = width // 2
    heads = half // HEAD_DIM
    total = 2 * rows
    nseq = lax.axis_size("seq")
    pairs = nseq // 2
    depth = (rows // BLOCK).bit_length() - 1
    levels = min(MAX_LEVELS, depth + nseq.bit_length() - 2)
    local = depth + 1
    far = levels - local + 1
    coarse = sum(total >> l for l in range(1, local))
    bf16 = jnp.bfloat16
    dma = pltpu.SemaphoreType.DMA
    return pl.pallas_call(
        functools.partial(kernel, pairs, levels, local),
        out_shape=jax.ShapeDtypeStruct((rows, width), bf16),
        in_specs=[pl.BlockSpec(memory_space=pl.ANY)] * 3,
        out_specs=pl.BlockSpec(memory_space=pl.ANY),
        scratch_shapes=[
            pltpu.VMEM((2, total + 2 * BLOCK, half), bf16),
            pltpu.VMEM((total, half), bf16),
            pltpu.VMEM((total, half), bf16),
            pltpu.VMEM((2, coarse, half), bf16),
            pltpu.VMEM((far, 2, BLOCK, half), bf16),
            pltpu.VMEM((far, 2, BLOCK, half), bf16),
            pltpu.VMEM((levels, 3, total, HEAD_DIM), jnp.float32),
            dma((3,)),
            dma((2, heads)),
            dma((2, heads)),
            dma((heads,)),
            dma((heads,)),
            dma((2, heads)),
            dma((2, heads)),
            dma((far, heads)),
            dma((far, heads)),
            dma((heads,)),
            dma((heads,)),
            dma((heads,)),
        ],
        compiler_params=pltpu.CompilerParams(
            collective_id=0, has_side_effects=True, vmem_limit_bytes=40 * 2**20
        ),
    )(queries, keys, values)


def solution(mesh):
    spec = P(("groups", "seq"), "head")
    return jax.shard_map(
        on_device, mesh=mesh, in_specs=(spec, spec, spec), out_specs=spec, check_vma=False
    )
```

```python
import functools
import math

import jax
import jax.numpy as jnp
from jax import lax
from jax.experimental import pallas as pl
from jax.experimental.pallas import tpu as pltpu
from jax.sharding import PartitionSpec as P

HEAD_DIM = 128
BLOCK = 128
MAX_LEVELS = 7
MESH = pl.DeviceIdType.MESH
RATE = math.log2(math.e) / math.sqrt(HEAD_DIM)


def score(query, key):
    return lax.dot_general(
        query, key, (((1,), (1,)), ((), ())), preferred_element_type=jnp.float32
    )


def kernel(
    pairs, levels, local, q_in, k_in, v_in, out, kv, qbuf, obuf, kv1, own, sib,
    state, load_sem, kv_send, kv_recv, q_send, q_recv, halo_send, halo_recv,
    lev_send, lev_recv, out_local, out_send, out_recv,
):
    rows, width = q_in.shape
    half = width // 2
    heads = half // HEAD_DIM
    total = 2 * rows
    blocks = total // BLOCK
    place = lax.axis_index("seq")
    side = lax.rem(place, 2)
    other = 1 - side
    pair = place // 2
    partner = {"seq": pair * 2 + other}
    first, last = pair == 0, pair == pairs - 1
    below = {"seq": jnp.maximum(pair - 1, 0) * 2 + side}
    above = {"seq": jnp.minimum(pair + 1, pairs - 1) * 2 + side}

    def mirror(level):
        apart = 1 << (level - local)
        bit = lax.rem(pair // apart, 2)
        return {"seq": (pair + apart - 2 * apart * bit) * 2 + side}

    barrier = pltpu.get_barrier_semaphore()

    def greet(peer):
        pl.semaphore_signal(barrier, inc=1, device_id=peer, device_id_type=MESH)

    greet(partner)
    pl.when(jnp.logical_not(first))(lambda: greet(below))
    pl.when(jnp.logical_not(last))(lambda: greet(above))
    for level in range(local + 1, levels + 1):
        greet(mirror(level))

    mine = pl.ds(pl.multiple_of(side * half, half), half)
    own_rows = pl.ds(pl.multiple_of(BLOCK + side * rows, BLOCK), rows)
    q_rows = pl.ds(pl.multiple_of(side * rows, BLOCK), rows)
    loads = [
        pltpu.make_async_copy(k_in.at[:, mine], kv.at[0, own_rows], load_sem.at[0]),
        pltpu.make_async_copy(v_in.at[:, mine], kv.at[1, own_rows], load_sem.at[1]),
        pltpu.make_async_copy(q_in.at[:, mine], qbuf.at[q_rows], load_sem.at[2]),
    ]
    for load in loads:
        load.start()
    sides = jnp.where(first, 0, 1) + jnp.where(last, 0, 1)
    pl.semaphore_wait(barrier, 1 + levels - local + sides)

    def lanes(h):
        return pl.ds(pl.multiple_of(h * HEAD_DIM, HEAD_DIM), HEAD_DIM)

    def remote(src, dst, send, recv, device):
        return pltpu.make_async_remote_copy(
            src_ref=src, dst_ref=dst, send_sem=send, recv_sem=recv,
            device_id=device, device_id_type=MESH,
        )

    def theirs(h):
        return pl.ds(pl.multiple_of(other * half + h * HEAD_DIM, HEAD_DIM), HEAD_DIM)

    def send_k(h):
        return remote(k_in.at[:, theirs(h)], kv.at[0, own_rows, lanes(h)],
                      kv_send.at[0, h], kv_recv.at[0, h], partner)

    def send_v(h):
        return remote(v_in.at[:, theirs(h)], kv.at[1, own_rows, lanes(h)],
                      kv_send.at[1, h], kv_recv.at[1, h], partner)

    def send_q(h):
        return remote(q_in.at[:, theirs(h)], qbuf.at[q_rows, lanes(h)],
                      q_send.at[h], q_recv.at[h], partner)

    def send_down(h):
        return remote(kv.at[:, pl.ds(BLOCK, BLOCK), lanes(h)],
                      kv.at[:, pl.ds(BLOCK + total, BLOCK), lanes(h)],
                      halo_send.at[0, h], halo_recv.at[0, h], below)

    def send_up(h):
        return remote(kv.at[:, pl.ds(total, BLOCK), lanes(h)],
                      kv.at[:, pl.ds(0, BLOCK), lanes(h)],
                      halo_send.at[1, h], halo_recv.at[1, h], above)

    def send_level(level, h):
        at = level - local
        return remote(own.at[at, :, :, lanes(h)], sib.at[at, :, :, lanes(h)],
                      lev_send.at[at, h], lev_recv.at[at, h], mirror(level))

    def keep_out(h):
        cols = pl.ds(pl.multiple_of(side * half + h * HEAD_DIM, HEAD_DIM), HEAD_DIM)
        return pltpu.make_async_copy(
            obuf.at[q_rows, lanes(h)], out.at[:, cols], out_local.at[h])

    def send_out(h):
        cols = pl.ds(pl.multiple_of(side * half + h * HEAD_DIM, HEAD_DIM), HEAD_DIM)
        far = pl.ds(pl.multiple_of(other * rows, BLOCK), rows)
        return remote(obuf.at[far, lanes(h)], out.at[:, cols],
                      out_send.at[h], out_recv.at[h], partner)

    def each(body):
        @pl.loop(0, heads)
        def _(h):
            body(h)

    def start_kv(h):
        send_k(h).start()
        send_v(h).start()

    ahead = min(2, heads)
    for h in range(ahead):
        start_kv(h)

    @pl.when(first)
    def _():
        kv[:, pl.ds(0, BLOCK), :] = jnp.zeros((2, BLOCK, half), kv.dtype)

    @pl.when(last)
    def _():
        kv[:, pl.ds(BLOCK + total, BLOCK), :] = jnp.zeros((2, BLOCK, half), kv.dtype)

    loads[0].wait()
    loads[1].wait()

    def halo(h, here):
        @pl.when((side == here) & jnp.logical_not(first))
        def _():
            send_down(h).start()

        @pl.when((side == 1 - here) & jnp.logical_not(last))
        def _():
            send_up(h).start()

    each(lambda h: halo(h, 0))

    rowid = lax.broadcasted_iota(jnp.int32, (BLOCK, 2 * BLOCK), 0)
    colid = lax.broadcasted_iota(jnp.int32, (BLOCK, 2 * BLOCK), 1)
    pairing = jnp.where((colid >> 1) == rowid, 1.0, 0.0).astype(jnp.bfloat16)

    def pair_sum(x):
        count = x.shape[0]
        parts = []
        for at in range(0, count, 2 * BLOCK):
            size = min(2 * BLOCK, count - at)
            parts.append(
                jnp.dot(pairing[: size // 2, :size], x[at : at + size],
                        preferred_element_type=jnp.float32).astype(jnp.bfloat16)
            )
        return parts[0] if len(parts) == 1 else jnp.concatenate(parts, axis=0)

    def coarsen(h):
        send_k(h).wait_recv()
        send_v(h).wait_recv()

        @pl.when(h + ahead < heads)
        def _():
            start_kv(h + ahead)

        @pl.when(h + ahead >= heads)
        def _():
            for i in range(2):
                send_q(2 * (h + ahead - heads) + i).start()

        halo(h, 1)
        both = jnp.concatenate(
            [kv[0, pl.ds(BLOCK, total), lanes(h)], kv[1, pl.ds(BLOCK, total), lanes(h)]],
            axis=1)
        offset = 0
        for level in range(1, local):
            both = pair_sum(both)
            count = total >> level
            for t in range(2):
                kv1[t, pl.ds(offset, count), lanes(h)] = both[:, t * HEAD_DIM : (t + 1) * HEAD_DIM]
            offset += count
        both = pair_sum(both)
        for t in range(2):
            own[0, t, :, lanes(h)] = both[:, t * HEAD_DIM : (t + 1) * HEAD_DIM]
        send_level(local, h).start()

    each(coarsen)

    for level in range(local, levels):
        at = level - local

        def climb(h, level=level, at=at):
            send_level(level, h).wait_recv()
            for t in range(2):
                joined = jnp.concatenate([own[at, t, :, lanes(h)], sib[at, t, :, lanes(h)]], axis=0)
                own[at + 1, t, :, lanes(h)] = pair_sum(joined)
            send_level(level + 1, h).start()

        each(climb)

    loads[2].wait()

    def attend(h):
        send_q(h).wait_recv()
        send_level(levels, h).wait_recv()

        @pl.when(jnp.logical_not(last))
        def _():
            send_down(h).wait_recv()

        @pl.when(jnp.logical_not(first))
        def _():
            send_up(h).wait_recv()

        queries = [qbuf[:, lanes(h)]]
        for level in range(1, levels + 1):
            queries.append(pair_sum(queries[-1]))

        def part(level, query, key, value, start, edge=None):
            size = query.shape[0]
            rate = RATE * 0.25**level
            scores = score(query, key)
            if edge is not None:
                column, missing = edge
                pieces = [scores[:, c : c + BLOCK] for c in range(0, scores.shape[1], BLOCK)]
                pieces[column] = jnp.where(missing, -1e30, pieces[column])
                scores = jnp.concatenate(pieces, axis=1)
            top = jnp.max(scores, axis=1, keepdims=True) * rate
            if level < levels:
                span = pl.ds(start, size)
                coarse_top = state[level, 0, span, :]
                highest = jnp.maximum(jnp.broadcast_to(top, (size, HEAD_DIM)), coarse_top)
                weight = jnp.exp2(coarse_top - highest)
            else:
                highest = jnp.broadcast_to(top, (size, HEAD_DIM))
            wide = jnp.concatenate([highest] * (key.shape[0] // BLOCK), axis=1)
            probs = jnp.exp2(scores * rate - wide).astype(jnp.bfloat16)
            ones = jnp.full_like(value, 2.0**level)
            both = jnp.dot(probs, jnp.concatenate([value, ones], axis=1),
                           preferred_element_type=jnp.float32)
            num, den = both[:, :HEAD_DIM], both[:, HEAD_DIM:]
            if level < levels:
                den = den + weight * state[level, 1, span, :]
                num = num + weight * state[level, 2, span, :]
            if level == 0:
                obuf[pl.ds(start, size), lanes(h)] = (num / den).astype(obuf.dtype)
            else:
                for at, x in enumerate((highest, den, num)):
                    for odd in range(2):
                        state[level - 1, at, pl.ds(2 * start + odd, size, stride=2), :] = x

        for level in range(levels, local - 1, -1):
            at = level - local
            part(level, queries[level], sib[at, 0, :, lanes(h)], sib[at, 1, :, lanes(h)], 0)
        for level in range(local - 1, 0, -1):
            offset = sum(total >> l for l in range(1, level))
            for b in range((total >> level) // BLOCK):
                near = pl.ds(offset + (b ^ 1) * BLOCK, BLOCK)
                part(level, queries[level][b * BLOCK : (b + 1) * BLOCK],
                     kv1[0, near, lanes(h)], kv1[1, near, lanes(h)], b * BLOCK)
        for b in range(blocks):
            window = pl.ds(b * BLOCK, 3 * BLOCK)
            edge = (0, first) if b == 0 else (2, last) if b == blocks - 1 else None
            part(0, queries[0][b * BLOCK : (b + 1) * BLOCK],
                 kv[0, window, lanes(h)], kv[1, window, lanes(h)], b * BLOCK, edge)
        keep_out(h).start()
        send_out(h).start()

    each(attend)

    def finish(h):
        send_k(h).wait_send()
        send_v(h).wait_send()
        send_q(h).wait_send()
        for level in range(local, levels + 1):
            send_level(level, h).wait_send()

        @pl.when(jnp.logical_not(first))
        def _():
            send_down(h).wait_send()

        @pl.when(jnp.logical_not(last))
        def _():
            send_up(h).wait_send()

        keep_out(h).wait()
        send_out(h).wait()

    each(finish)


def on_device(queries, keys, values):
    rows, width = queries.shape
    half = width // 2
    heads = half // HEAD_DIM
    total = 2 * rows
    nseq = lax.axis_size("seq")
    pairs = nseq // 2
    depth = (rows // BLOCK).bit_length() - 1
    levels = min(MAX_LEVELS, depth + nseq.bit_length() - 2)
    local = depth + 1
    far = levels - local + 1
    coarse = sum(total >> l for l in range(1, local))
    bf16 = jnp.bfloat16
    dma = pltpu.SemaphoreType.DMA
    return pl.pallas_call(
        functools.partial(kernel, pairs, levels, local),
        out_shape=jax.ShapeDtypeStruct((rows, width), bf16),
        in_specs=[pl.BlockSpec(memory_space=pl.ANY)] * 3,
        out_specs=pl.BlockSpec(memory_space=pl.ANY),
        scratch_shapes=[
            pltpu.VMEM((2, total + 2 * BLOCK, half), bf16),
            pltpu.VMEM((total, half), bf16),
            pltpu.VMEM((total, half), bf16),
            pltpu.VMEM((2, coarse, half), bf16),
            pltpu.VMEM((far, 2, BLOCK, half), bf16),
            pltpu.VMEM((far, 2, BLOCK, half), bf16),
            pltpu.VMEM((levels, 3, total, HEAD_DIM), jnp.float32),
            dma((3,)),
            dma((2, heads)),
            dma((2, heads)),
            dma((heads,)),
            dma((heads,)),
            dma((2, heads)),
            dma((2, heads)),
            dma((far, heads)),
            dma((far, heads)),
            dma((heads,)),
            dma((heads,)),
            dma((heads,)),
        ],
        compiler_params=pltpu.CompilerParams(
            collective_id=0, has_side_effects=True, vmem_limit_bytes=63 * 2**20
        ),
    )(queries, keys, values)


def solution(mesh):
    spec = P(("groups", "seq"), "head")
    return jax.shard_map(
        on_device, mesh=mesh, in_specs=(spec, spec, spec), out_specs=spec, check_vma=False
    )
```

```python
import functools
import math

import jax
import jax.numpy as jnp
from jax import lax
from jax.experimental import pallas as pl
from jax.experimental.pallas import tpu as pltpu
from jax.sharding import PartitionSpec as P

HEAD_DIM = 128
BLOCK = 128
MAX_LEVELS = 7
MESH = pl.DeviceIdType.MESH
RATE = math.log2(math.e) / math.sqrt(HEAD_DIM)


def score(query, key):
    return lax.dot_general(
        query, key, (((1,), (1,)), ((), ())), preferred_element_type=jnp.float32
    )


def kernel(
    pairs, levels, local, q_in, k_in, v_in, out, kv, qbuf, obuf, kv1, own, sib,
    state, load_sem, kv_send, kv_recv, q_send, q_recv, halo_send, halo_recv,
    lev_send, lev_recv, out_local, out_send, out_recv,
):
    rows, width = q_in.shape
    half = width // 2
    heads = half // HEAD_DIM
    total = 2 * rows
    blocks = total // BLOCK
    place = lax.axis_index("seq")
    side = lax.rem(place, 2)
    other = 1 - side
    pair = place // 2
    partner = {"seq": pair * 2 + other}
    first, last = pair == 0, pair == pairs - 1
    below = {"seq": jnp.maximum(pair - 1, 0) * 2 + side}
    above = {"seq": jnp.minimum(pair + 1, pairs - 1) * 2 + side}

    def mirror(level):
        apart = 1 << (level - local)
        bit = lax.rem(pair // apart, 2)
        return {"seq": (pair + apart - 2 * apart * bit) * 2 + side}

    barrier = pltpu.get_barrier_semaphore()

    def greet(peer):
        pl.semaphore_signal(barrier, inc=1, device_id=peer, device_id_type=MESH)

    greet(partner)
    pl.when(jnp.logical_not(first))(lambda: greet(below))
    pl.when(jnp.logical_not(last))(lambda: greet(above))
    for level in range(local + 1, levels + 1):
        greet(mirror(level))

    mine = pl.ds(pl.multiple_of(side * half, half), half)
    own_rows = pl.ds(pl.multiple_of(BLOCK + side * rows, BLOCK), rows)
    q_rows = pl.ds(pl.multiple_of(side * rows, BLOCK), rows)
    loads = [
        pltpu.make_async_copy(k_in.at[:, mine], kv.at[0, own_rows], load_sem.at[0]),
        pltpu.make_async_copy(v_in.at[:, mine], kv.at[1, own_rows], load_sem.at[1]),
        pltpu.make_async_copy(q_in.at[:, mine], qbuf.at[q_rows], load_sem.at[2]),
    ]
    for load in loads:
        load.start()
    sides = jnp.where(first, 0, 1) + jnp.where(last, 0, 1)
    pl.semaphore_wait(barrier, 1 + levels - local + sides)

    def lanes(h):
        return pl.ds(pl.multiple_of(h * HEAD_DIM, HEAD_DIM), HEAD_DIM)

    def remote(src, dst, send, recv, device):
        return pltpu.make_async_remote_copy(
            src_ref=src, dst_ref=dst, send_sem=send, recv_sem=recv,
            device_id=device, device_id_type=MESH,
        )

    def theirs(h):
        return pl.ds(pl.multiple_of(other * half + h * HEAD_DIM, HEAD_DIM), HEAD_DIM)

    def send_k(h):
        return remote(k_in.at[:, theirs(h)], kv.at[0, own_rows, lanes(h)],
                      kv_send.at[0, h], kv_recv.at[0, h], partner)

    def send_v(h):
        return remote(v_in.at[:, theirs(h)], kv.at[1, own_rows, lanes(h)],
                      kv_send.at[1, h], kv_recv.at[1, h], partner)

    def send_q(h):
        return remote(q_in.at[:, theirs(h)], qbuf.at[q_rows, lanes(h)],
                      q_send.at[h], q_recv.at[h], partner)

    def send_down(h):
        return remote(kv.at[:, pl.ds(BLOCK, BLOCK), lanes(h)],
                      kv.at[:, pl.ds(BLOCK + total, BLOCK), lanes(h)],
                      halo_send.at[0, h], halo_recv.at[0, h], below)

    def send_up(h):
        return remote(kv.at[:, pl.ds(total, BLOCK), lanes(h)],
                      kv.at[:, pl.ds(0, BLOCK), lanes(h)],
                      halo_send.at[1, h], halo_recv.at[1, h], above)

    def send_level(level, h):
        at = level - local
        return remote(own.at[at, :, :, lanes(h)], sib.at[at, :, :, lanes(h)],
                      lev_send.at[at, h], lev_recv.at[at, h], mirror(level))

    def keep_out(h):
        cols = pl.ds(pl.multiple_of(side * half + h * HEAD_DIM, HEAD_DIM), HEAD_DIM)
        return pltpu.make_async_copy(
            obuf.at[q_rows, lanes(h)], out.at[:, cols], out_local.at[h])

    def send_out(h):
        cols = pl.ds(pl.multiple_of(side * half + h * HEAD_DIM, HEAD_DIM), HEAD_DIM)
        far = pl.ds(pl.multiple_of(other * rows, BLOCK), rows)
        return remote(obuf.at[far, lanes(h)], out.at[:, cols],
                      out_send.at[h], out_recv.at[h], partner)

    def each(body):
        @pl.loop(0, heads)
        def _(h):
            body(h)

    def start_kv(h):
        send_k(h).start()
        send_v(h).start()

    ahead = min(2, heads)
    for h in range(ahead):
        start_kv(h)

    @pl.when(first)
    def _():
        kv[:, pl.ds(0, BLOCK), :] = jnp.zeros((2, BLOCK, half), kv.dtype)

    @pl.when(last)
    def _():
        kv[:, pl.ds(BLOCK + total, BLOCK), :] = jnp.zeros((2, BLOCK, half), kv.dtype)

    loads[0].wait()
    loads[1].wait()

    def halo(h, here):
        @pl.when((side == here) & jnp.logical_not(first))
        def _():
            send_down(h).start()

        @pl.when((side == 1 - here) & jnp.logical_not(last))
        def _():
            send_up(h).start()

    each(lambda h: halo(h, 0))

    rowid = lax.broadcasted_iota(jnp.int32, (BLOCK, 2 * BLOCK), 0)
    colid = lax.broadcasted_iota(jnp.int32, (BLOCK, 2 * BLOCK), 1)
    pairing = jnp.where((colid >> 1) == rowid, 1.0, 0.0).astype(jnp.bfloat16)

    def pair_sum(x):
        count = x.shape[0]
        parts = []
        for at in range(0, count, 2 * BLOCK):
            size = min(2 * BLOCK, count - at)
            parts.append(
                jnp.dot(pairing[: size // 2, :size], x[at : at + size],
                        preferred_element_type=jnp.float32).astype(jnp.bfloat16)
            )
        return parts[0] if len(parts) == 1 else jnp.concatenate(parts, axis=0)

    def coarsen(h):
        send_k(h).wait_recv()
        send_v(h).wait_recv()

        @pl.when(h + ahead < heads)
        def _():
            start_kv(h + ahead)

        @pl.when(h + ahead >= heads)
        def _():
            for i in range(2):
                send_q(2 * (h + ahead - heads) + i).start()

        halo(h, 1)
        both = jnp.concatenate(
            [kv[0, pl.ds(BLOCK, total), lanes(h)], kv[1, pl.ds(BLOCK, total), lanes(h)]],
            axis=1)
        offset = 0
        for level in range(1, local):
            both = pair_sum(both)
            count = total >> level
            for t in range(2):
                kv1[t, pl.ds(offset, count), lanes(h)] = both[:, t * HEAD_DIM : (t + 1) * HEAD_DIM]
            offset += count
        both = pair_sum(both)
        for t in range(2):
            own[0, t, :, lanes(h)] = both[:, t * HEAD_DIM : (t + 1) * HEAD_DIM]
        send_level(local, h).start()

    def climb(level, h):
        at = level - local
        send_level(level, h).wait_recv()
        for t in range(2):
            joined = jnp.concatenate([own[at, t, :, lanes(h)], sib[at, t, :, lanes(h)]], axis=0)
            own[at + 1, t, :, lanes(h)] = pair_sum(joined)
        send_level(level + 1, h).start()

    @pl.loop(0, heads + levels - local)
    def _(step):
        pl.when(step < heads)(lambda: coarsen(step))
        for level in range(local, levels):
            h = step - (level - local + 1)
            pl.when((h >= 0) & (h < heads))(functools.partial(climb, level, h))

    loads[2].wait()

    def attend(h):
        send_q(h).wait_recv()
        send_level(levels, h).wait_recv()

        @pl.when(jnp.logical_not(last))
        def _():
            send_down(h).wait_recv()

        @pl.when(jnp.logical_not(first))
        def _():
            send_up(h).wait_recv()

        queries = [qbuf[:, lanes(h)]]
        for level in range(1, levels + 1):
            queries.append(pair_sum(queries[-1]))

        def part(level, query, key, value, start, edge=None):
            size = query.shape[0]
            rate = RATE * 0.25**level
            scores = score(query, key)
            if edge is not None:
                column, missing = edge
                pieces = [scores[:, c : c + BLOCK] for c in range(0, scores.shape[1], BLOCK)]
                pieces[column] = jnp.where(missing, -1e30, pieces[column])
                scores = jnp.concatenate(pieces, axis=1)
            top = jnp.max(scores, axis=1, keepdims=True) * rate
            if level < levels:
                span = pl.ds(start, size)
                coarse_top = state[level, 0, span, :]
                highest = jnp.maximum(jnp.broadcast_to(top, (size, HEAD_DIM)), coarse_top)
                weight = jnp.exp2(coarse_top - highest)
            else:
                highest = jnp.broadcast_to(top, (size, HEAD_DIM))
            wide = jnp.concatenate([highest] * (key.shape[0] // BLOCK), axis=1)
            probs = jnp.exp2(scores * rate - wide).astype(jnp.bfloat16)
            ones = jnp.full_like(value, 2.0**level)
            both = jnp.dot(probs, jnp.concatenate([value, ones], axis=1),
                           preferred_element_type=jnp.float32)
            num, den = both[:, :HEAD_DIM], both[:, HEAD_DIM:]
            if level < levels:
                den = den + weight * state[level, 1, span, :]
                num = num + weight * state[level, 2, span, :]
            if level == 0:
                obuf[pl.ds(start, size), lanes(h)] = (num / den).astype(obuf.dtype)
            else:
                for at, x in enumerate((highest, den, num)):
                    for odd in range(2):
                        state[level - 1, at, pl.ds(2 * start + odd, size, stride=2), :] = x

        for level in range(levels, local - 1, -1):
            at = level - local
            part(level, queries[level], sib[at, 0, :, lanes(h)], sib[at, 1, :, lanes(h)], 0)
        for level in range(local - 1, 0, -1):
            offset = sum(total >> l for l in range(1, level))
            for b in range((total >> level) // BLOCK):
                near = pl.ds(offset + (b ^ 1) * BLOCK, BLOCK)
                part(level, queries[level][b * BLOCK : (b + 1) * BLOCK],
                     kv1[0, near, lanes(h)], kv1[1, near, lanes(h)], b * BLOCK)
        for b in range(blocks):
            window = pl.ds(b * BLOCK, 3 * BLOCK)
            edge = (0, first) if b == 0 else (2, last) if b == blocks - 1 else None
            part(0, queries[0][b * BLOCK : (b + 1) * BLOCK],
                 kv[0, window, lanes(h)], kv[1, window, lanes(h)], b * BLOCK, edge)
        keep_out(h).start()
        send_out(h).start()

    each(attend)

    def finish(h):
        send_k(h).wait_send()
        send_v(h).wait_send()
        send_q(h).wait_send()
        for level in range(local, levels + 1):
            send_level(level, h).wait_send()

        @pl.when(jnp.logical_not(first))
        def _():
            send_down(h).wait_send()

        @pl.when(jnp.logical_not(last))
        def _():
            send_up(h).wait_send()

        keep_out(h).wait()
        send_out(h).wait()

    each(finish)


def on_device(queries, keys, values):
    rows, width = queries.shape
    half = width // 2
    heads = half // HEAD_DIM
    total = 2 * rows
    nseq = lax.axis_size("seq")
    pairs = nseq // 2
    depth = (rows // BLOCK).bit_length() - 1
    levels = min(MAX_LEVELS, depth + nseq.bit_length() - 2)
    local = depth + 1
    far = levels - local + 1
    coarse = sum(total >> l for l in range(1, local))
    bf16 = jnp.bfloat16
    dma = pltpu.SemaphoreType.DMA
    return pl.pallas_call(
        functools.partial(kernel, pairs, levels, local),
        out_shape=jax.ShapeDtypeStruct((rows, width), bf16),
        in_specs=[pl.BlockSpec(memory_space=pl.ANY)] * 3,
        out_specs=pl.BlockSpec(memory_space=pl.ANY),
        scratch_shapes=[
            pltpu.VMEM((2, total + 2 * BLOCK, half), bf16),
            pltpu.VMEM((total, half), bf16),
            pltpu.VMEM((total, half), bf16),
            pltpu.VMEM((2, coarse, half), bf16),
            pltpu.VMEM((far, 2, BLOCK, half), bf16),
            pltpu.VMEM((far, 2, BLOCK, half), bf16),
            pltpu.VMEM((levels, 3, total, HEAD_DIM), jnp.float32),
            dma((3,)),
            dma((2, heads)),
            dma((2, heads)),
            dma((heads,)),
            dma((heads,)),
            dma((2, heads)),
            dma((2, heads)),
            dma((far, heads)),
            dma((far, heads)),
            dma((heads,)),
            dma((heads,)),
            dma((heads,)),
        ],
        compiler_params=pltpu.CompilerParams(
            collective_id=0, has_side_effects=True, vmem_limit_bytes=63 * 2**20
        ),
    )(queries, keys, values)


def solution(mesh):
    spec = P(("groups", "seq"), "head")
    return jax.shard_map(
        on_device, mesh=mesh, in_specs=(spec, spec, spec), out_specs=spec, check_vma=False
    )
```
